512 devices in a mesh: heads: 16 (over y, core), seq: 32 (over z, x).
Axes of the slice: x: 4, y: 8, z: 8, core: 2. Of those that a mesh axis runs over, the one named last changes fastest.
Arguments:
- queries: bfloat16 [8192, 4096], P('seq', 'heads'), may hold values from -6 to 6
- keys: bfloat16 [8192, 4096], P('seq', 'heads'), may hold values from -6 to 6
- values: bfloat16 [8192, 4096], P('seq', 'heads'), may hold values from -6 to 6
- src_keys: bfloat16 [4096, 4096], P('seq', 'heads'), may hold values from -6 to 6
- src_values: bfloat16 [4096, 4096], P('seq', 'heads'), may hold values from -6 to 6
- norm_gain: float32 [4096], P('heads'), may hold values from 0.1 to 1.9
- out_weight: bfloat16 [4096, 4096], P('heads'), may hold values from -0.09375 to 0.09375
- grad_out: bfloat16 [8192, 4096], P('seq', 'heads'), may hold values from -6 to 6
Outputs:
- attended: bfloat16 [8192, 4096], P('seq', 'heads')
- grad_queries: bfloat16 [8192, 4096], P('seq', 'heads')
- grad_keys: bfloat16 [8192, 4096], P('seq', 'heads')
- grad_values: bfloat16 [8192, 4096], P('seq', 'heads')
- grad_src_keys: bfloat16 [4096, 4096], P('seq', 'heads')
- grad_src_values: bfloat16 [4096, 4096], P('seq', 'heads')
- grad_gain: float32 [4096], P('heads')
The draws below stay inside these ranges and needn't reach their ends.
All inputs are finite; a program needn't handle non-finite values.
Results may differ from the reference program's by a relative error of at most 0.00115.
Values may be sent and summed in bfloat16 or wider, within the bound.
No kernel may reach another device: no remote copies, remote signals or barrier semaphores. Data moves between devices by JAX's collectives and lax.ppermute only.
A program may use at most 64 MiB of HBM per device.

```python
import math
import jax
import jax.numpy as jnp
from jax import lax

D = 4096
DH = 128
TGT_DEV = 256
HEADS = 32
TGT = 8192
SRC = 4096
N_SEQ = 32


def levels(own_key, shape, split, low, high):
    def one(axis_at, blocks):
        heights = jax.random.uniform(jax.random.fold_in(jax.random.fold_in(own_key, 6), axis_at), (blocks,), jnp.float32, low / len(split), high / len(split))
        return jnp.repeat(jnp.exp(heights), shape[axis_at] // blocks).reshape((-1,) + (1,) * (len(shape) - axis_at - 1))

    gain = one(*split[0])
    for cut in split[1:]:
        gain = gain * one(*cut)
    return gain


def noise(rng, shape, spread, most, shards=(), held_as=jnp.bfloat16):
    entries = spread * jax.random.normal(rng, shape, jnp.float32)
    if shards:
        entries = entries * levels(rng, shape, shards, -0.22, 0.18)
    return jnp.clip(entries, -most, most).astype(held_as)


def setup_inputs(seed: int = 0) -> dict:
    arg_keys = jax.random.split(jax.random.key(seed), 9)
    queries = noise(arg_keys[0], (TGT, HEADS * DH), 1.0, 6.0, ((0, 32), (1, 16)))
    keys = noise(arg_keys[1], (TGT, HEADS * DH), 1.0, 6.0, ((0, 32), (1, 16)))
    values = noise(arg_keys[2], (TGT, HEADS * DH), 1.0, 6.0, ((0, 32), (1, 16)))
    src_keys = noise(arg_keys[3], (SRC, HEADS * DH), 1.0, 6.0, ((0, 32), (1, 16)))
    src_values = noise(arg_keys[4], (SRC, HEADS * DH), 1.0, 6.0, ((0, 32), (1, 16)))
    norm_gain = jnp.clip(1.0 + 0.18 * jax.random.normal(arg_keys[5], (HEADS * DH,), jnp.float32), 0.1, 1.9)
    out_weight = noise(arg_keys[6], (HEADS * DH, D), (HEADS * DH) ** -0.5, 0.09375, ((0, 16),))
    grad_out = noise(arg_keys[7], (TGT, D), 1.0, 6.0, ((0, 32), (1, 16)))
    return {"queries": queries, "keys": keys, "values": values, "src_keys": src_keys, "src_values": src_values, "norm_gain": norm_gain, "out_weight": out_weight, "grad_out": grad_out}


highest = lax.Precision.HIGHEST

def outer_sum(key_rows, value_rows):
    return jnp.einsum('shd,she->hde', key_rows, value_rows, precision=highest)

def block_attend(query_rows, key_rows, value_rows, before, source_state, gain_rows, self_scale, cross_scale):
    length = query_rows.shape[0]
    scores = jnp.einsum('thd,shd->hts', query_rows, key_rows, precision=highest)
    causal = (lax.broadcasted_iota(jnp.int32, (length, length), 0) >= lax.broadcasted_iota(jnp.int32, (length, length), 1)).astype(jnp.float32)
    within = jnp.einsum('hts,she->the', scores * causal[None], value_rows, precision=highest)
    earlier = jnp.einsum('thd,hde->the', query_rows, before, precision=highest)
    crossed = jnp.einsum('thd,hde->the', query_rows, source_state, precision=highest)
    mixture = (within + earlier) * self_scale + crossed * cross_scale
    return mixture * lax.rsqrt(lax.optimization_barrier(jnp.mean(mixture * mixture, axis=-1, keepdims=True)) + 1e-06) * gain_rows[None]

def reference(queries, keys, values, src_keys, src_values, norm_gain, out_weight, grad_out):
    self_scale = 1.0 / math.sqrt(DH * TGT)
    cross_scale = 1.0 / math.sqrt(DH * SRC)

    def split_rows(array, rows):
        return array.astype(jnp.float32).reshape(rows, HEADS, DH)

    def forward(query_all, key_all, value_all, src_key_all, src_value_all, gain_rows):
        source_state = outer_sum(src_key_all, src_value_all)

        def blocked(array):
            return array.reshape(N_SEQ, TGT_DEV, HEADS, DH)

        def advance(state, pieces):
            query_rows, key_rows, value_rows = pieces
            result = block_attend(query_rows, key_rows, value_rows, state, source_state, gain_rows, self_scale, cross_scale)
            return (state + outer_sum(key_rows, value_rows), result)
        initial = jnp.zeros((HEADS, DH, DH), jnp.float32)
        ending, results = lax.scan(advance, initial, (blocked(query_all), blocked(key_all), blocked(value_all)))
        return results.reshape(TGT, HEADS, DH)
    normed, pull = jax.vjp(forward, split_rows(queries, TGT), split_rows(keys, TGT), split_rows(values, TGT), split_rows(src_keys, SRC), split_rows(src_values, SRC), norm_gain.reshape(HEADS, DH))
    grad_normed = jnp.dot(grad_out, out_weight.T, preferred_element_type=jnp.float32).reshape(TGT, HEADS, DH)
    grads = pull(grad_normed)
    width = HEADS * DH
    return (normed.reshape(TGT, width).astype(jnp.bfloat16), grads[0].reshape(TGT, width).astype(jnp.bfloat16), grads[1].reshape(TGT, width).astype(jnp.bfloat16), grads[2].reshape(TGT, width).astype(jnp.bfloat16), grads[3].reshape(SRC, width).astype(jnp.bfloat16), grads[4].reshape(SRC, width).astype(jnp.bfloat16), grads[5].reshape(width))
```

```python
import functools
import math

import jax
import jax.numpy as jnp
from jax import lax
from jax.experimental import pallas as pl
from jax.experimental.pallas import tpu as pltpu
from jax.sharding import PartitionSpec as P

DH = 128
f32 = jnp.float32
bf16 = jnp.bfloat16
MIB = 1024 * 1024


def dot(a, b, over_a, over_b):
    return lax.dot_general(a, b, (((over_a,), (over_b,)), ((), ())), preferred_element_type=f32)


def halves(x):
    high = x.astype(bf16)
    return high, (x - high.astype(f32)).astype(bf16)


def head(h):
    return slice(h * DH, (h + 1) * DH)


def states_kernel(k_ref, v_ref, sk_ref, sv_ref, out_ref, *, heads, rows):
    per = DH // rows
    for h in range(heads):
        own = dot(k_ref[:, head(h)], v_ref[:, head(h)], 0, 0)
        source = dot(sk_ref[:, head(h)], sv_ref[:, head(h)], 0, 0)
        out_ref[h * per : (h + 1) * per, :rows, :] = own.reshape(per, rows, DH)
        out_ref[h * per : (h + 1) * per, rows:, :] = source.reshape(per, rows, DH)


def prefix_kernel(in_ref, out_ref, *, count, rows, self_scale, cross_scale):
    total = in_ref[0, rows:, :]
    for j in range(1, count):
        total = total + in_ref[j, rows:, :]
    state = total * cross_scale
    for j in range(count):
        out_ref[j] = state
        state = state + in_ref[j, :rows, :] * self_scale


def forward_kernel(q_ref, k_ref, v_ref, c_ref, gain_ref, att_ref, mix_ref, high_ref, low_ref, *, heads, self_scale):
    length = q_ref.shape[0]
    causal = lax.broadcasted_iota(jnp.int32, (length, length), 0) >= lax.broadcasted_iota(jnp.int32, (length, length), 1)
    for h in range(heads):
        q, k, v = q_ref[:, head(h)], k_ref[:, head(h)], v_ref[:, head(h)]
        masked = jnp.where(causal, dot(q, k, 1, 1), 0.0) * self_scale
        high, low = halves(masked)
        high_ref[h] = high
        low_ref[h] = low
        c_high, c_low = halves(c_ref[head(h), :])
        mixture = dot(high, v, 1, 0) + dot(low, v, 1, 0) + dot(q, c_high, 1, 0) + dot(q, c_low, 1, 0)
        mix_ref[:, head(h)] = mixture
        inverse = lax.rsqrt(jnp.mean(mixture * mixture, axis=-1, keepdims=True) + 1e-06)
        att_ref[:, head(h)] = (mixture * inverse * gain_ref[h : h + 1, :]).astype(bf16)


def cotangent_kernel(g_ref, w_ref, q_ref, mix_ref, gain_ref, out_ref, high_ref, low_ref, *, heads, rows, groups):
    width = g_ref.shape[2]
    grad_normed = dot(g_ref[0], w_ref[:, :width], 1, 1)
    for b in range(1, groups):
        grad_normed = grad_normed + dot(g_ref[b], w_ref[:, b * width : (b + 1) * width], 1, 1)
    per = DH // rows
    gains = []
    for h in range(heads):
        mixture = mix_ref[:, head(h)]
        inverse = lax.rsqrt(jnp.mean(mixture * mixture, axis=-1, keepdims=True) + 1e-06)
        part = grad_normed[:, head(h)]
        gains.append(jnp.sum(part * (mixture * inverse), axis=0, keepdims=True))
        gained = part * gain_ref[h : h + 1, :]
        inner = jnp.mean(gained * mixture, axis=-1, keepdims=True)
        grad_mixture = inverse * gained - mixture * (inverse * inverse * inverse * inner)
        high, low = halves(grad_mixture)
        high_ref[:, head(h)] = high
        low_ref[:, head(h)] = low
        q = q_ref[:, head(h)]
        outer = dot(q, high, 0, 0) + dot(q, low, 0, 0)
        out_ref[h * per : (h + 1) * per, :rows, :] = outer.reshape(per, rows, DH)
    gain = jnp.concatenate(gains + [jnp.zeros((rows - heads, DH), f32)], axis=0)
    out_ref[:, rows:, :] = jnp.broadcast_to(gain[None], (heads * per, rows, DH))


def local_kernel(q_ref, k_ref, v_ref, c_ref, mh_ref, ml_ref, gh_ref, gl_ref, gq_ref, gk_ref, gv_ref, *, heads, self_scale):
    length = q_ref.shape[0]
    causal = lax.broadcasted_iota(jnp.int32, (length, length), 0) >= lax.broadcasted_iota(jnp.int32, (length, length), 1)
    for h in range(heads):
        q, k, v = q_ref[:, head(h)], k_ref[:, head(h)], v_ref[:, head(h)]
        high, low = gh_ref[:, head(h)], gl_ref[:, head(h)]
        scores = jnp.where(causal, dot(high, v, 1, 1) + dot(low, v, 1, 1), 0.0) * self_scale
        s_high, s_low = halves(scores)
        c_high, c_low = halves(c_ref[head(h), :])
        m_high, m_low = mh_ref[h], ml_ref[h]
        grad_query = dot(s_high, k, 1, 0) + dot(s_low, k, 1, 0)
        grad_query = grad_query + dot(high, c_high, 1, 1) + dot(high, c_low, 1, 1) + dot(low, c_high, 1, 1)
        gq_ref[:, head(h)] = grad_query.astype(bf16)
        gk_ref[:, head(h)] = dot(s_high, q, 0, 0) + dot(s_low, q, 0, 0)
        gv_ref[:, head(h)] = dot(m_high, high, 0, 0) + dot(m_high, low, 0, 0) + dot(m_low, high, 0, 0)


def suffix_kernel(in_ref, out_ref, gain_ref, *, count, rows, heads, self_scale, cross_scale):
    gain = in_ref[0, rows:, :]
    for j in range(1, count):
        gain = gain + in_ref[j, rows:, :]
    gain_ref[...] = gain[:heads, :]
    state = jnp.zeros((rows, DH), f32)
    for j in range(count - 1, -1, -1):
        out_ref[j, :rows, :] = state * self_scale
        state = state + in_ref[j, :rows, :]
    total = state * cross_scale
    for j in range(count):
        out_ref[j, rows:, :] = total


def final_kernel(k_ref, v_ref, sk_ref, sv_ref, s_ref, gk_ref, gv_ref, out_k, out_v, out_sk, out_sv, *, heads, rows):
    per = DH // rows
    for h in range(heads):
        later = s_ref[h * per : (h + 1) * per, :rows, :].reshape(DH, DH)
        total = s_ref[h * per : (h + 1) * per, rows:, :].reshape(DH, DH)
        l_high, l_low = halves(later)
        t_high, t_low = halves(total)
        k, v, sk, sv = k_ref[:, head(h)], v_ref[:, head(h)], sk_ref[:, head(h)], sv_ref[:, head(h)]
        out_k[:, head(h)] = (gk_ref[:, head(h)] + dot(v, l_high, 1, 1) + dot(v, l_low, 1, 1)).astype(bf16)
        out_v[:, head(h)] = (gv_ref[:, head(h)] + dot(k, l_high, 1, 0) + dot(k, l_low, 1, 0)).astype(bf16)
        out_sk[:, head(h)] = (dot(sv, t_high, 1, 1) + dot(sv, t_low, 1, 1)).astype(bf16)
        out_sv[:, head(h)] = (dot(sk, t_high, 1, 0) + dot(sk, t_low, 1, 0)).astype(bf16)


def call(kernel, outs, name, **static):
    whole = pl.BlockSpec(memory_space=pltpu.VMEM)
    shapes = [jax.ShapeDtypeStruct(shape, dtype) for shape, dtype in outs]

    def run(*operands):
        return pl.pallas_call(
            functools.partial(kernel, **static),
            out_shape=shapes,
            in_specs=[whole] * len(operands),
            out_specs=[whole] * len(shapes),
            compiler_params=pltpu.CompilerParams(vmem_limit_bytes=24 * MIB),
            name=name,
        )(*operands)

    return run


def on_device(queries, keys, values, src_keys, src_values, norm_gain, out_weight, grad_out):
    length, width = queries.shape
    src_length = src_keys.shape[0]
    heads = width // DH
    count = lax.axis_size("seq")
    groups = lax.axis_size("heads")
    rows = width // count
    self_scale = 1.0 / math.sqrt(DH * length * count)
    cross_scale = 1.0 / math.sqrt(DH * src_length * count)
    gain = norm_gain.reshape(heads, DH)

    gathered = lax.all_gather(grad_out, "heads")
    (own,) = call(states_kernel, [((count, 2 * rows, DH), f32)], "states", heads=heads, rows=rows)(keys, values, src_keys, src_values)
    own = lax.all_to_all(own, "seq", 0, 0)
    (before,) = call(
        prefix_kernel, [((count, rows, DH), f32)], "prefix", count=count, rows=rows, self_scale=self_scale, cross_scale=cross_scale
    )(own)
    before = lax.all_to_all(before, "seq", 0, 0).reshape(width, DH)
    attended, mixture, m_high, m_low = call(
        forward_kernel,
        [((length, width), bf16), ((length, width), f32), ((heads, length, length), bf16), ((heads, length, length), bf16)],
        "forward",
        heads=heads,
        self_scale=self_scale,
    )(queries, keys, values, before, gain)
    outer, g_high, g_low = call(
        cotangent_kernel,
        [((count, 2 * rows, DH), f32), ((length, width), bf16), ((length, width), bf16)],
        "cotangent",
        heads=heads,
        rows=rows,
        groups=groups,
    )(gathered, out_weight, queries, mixture, gain)
    outer = lax.all_to_all(outer, "seq", 0, 0)
    grad_query, grad_key, grad_value = call(
        local_kernel,
        [((length, width), bf16), ((length, width), f32), ((length, width), f32)],
        "local",
        heads=heads,
        self_scale=self_scale,
    )(queries, keys, values, before, m_high, m_low, g_high, g_low)
    later, grad_gain = call(
        suffix_kernel,
        [((count, 2 * rows, DH), f32), ((heads, DH), f32)],
        "suffix",
        count=count,
        rows=rows,
        heads=heads,
        self_scale=self_scale,
        cross_scale=cross_scale,
    )(outer)
    later = lax.all_to_all(later, "seq", 0, 0)
    grad_key, grad_value, grad_src_key, grad_src_value = call(
        final_kernel,
        [((length, width), bf16), ((length, width), bf16), ((src_length, width), bf16), ((src_length, width), bf16)],
        "final",
        heads=heads,
        rows=rows,
    )(keys, values, src_keys, src_values, later, grad_key, grad_value)
    return attended, grad_query, grad_key, grad_value, grad_src_key, grad_src_value, grad_gain.reshape(width)


def solution(mesh):
    block = P("seq", "heads")
    return jax.shard_map(
        on_device,
        mesh=mesh,
        in_specs=(block, block, block, block, block, P("heads"), P("heads", None), block),
        out_specs=(block, block, block, block, block, block, P("heads")),
        check_vma=False,
    )
```

```python
import functools
import math

import jax
import jax.numpy as jnp
from jax import lax
from jax.experimental import pallas as pl
from jax.experimental.pallas import tpu as pltpu
from jax.sharding import PartitionSpec as P

DH = 128
f32 = jnp.float32
bf16 = jnp.bfloat16
MIB = 1024 * 1024


def dot(a, b, over_a, over_b):
    return lax.dot_general(a, b, (((over_a,), (over_b,)), ((), ())), preferred_element_type=f32)


def halves(x):
    high = x.astype(bf16)
    return high, (x - high.astype(f32)).astype(bf16)


def head(h):
    return slice(h * DH, (h + 1) * DH)


def states_kernel(k_hbm, v_hbm, sk_hbm, sv_hbm, out_ref, k_ref, v_ref, sk_ref, sv_ref, sems, *, heads, rows):
    pairs = ((k_hbm, k_ref), (v_hbm, v_ref), (sk_hbm, sk_ref), (sv_hbm, sv_ref))
    loads = [pltpu.make_async_copy(a, b, sems.at[i]) for i, (a, b) in enumerate(pairs)]
    for load in loads:
        load.start()
    per = DH // rows
    for at, left, right in ((0, k_ref, v_ref), (1, sk_ref, sv_ref)):
        loads[2 * at].wait()
        loads[2 * at + 1].wait()
        for h in range(heads):
            state = dot(left[:, head(h)], right[:, head(h)], 0, 0)
            out_ref[h * per : (h + 1) * per, at * rows : (at + 1) * rows, :] = state.reshape(per, rows, DH)


def pack_kernel(*refs):
    *parts, _, out_ref, sems = refs
    copies, at = [], 0
    for i, part in enumerate(parts):
        copies.append(pltpu.make_async_copy(part, out_ref.at[at : at + part.shape[0]], sems.at[i]))
        at += part.shape[0]
    for copy in copies:
        copy.start()
    for copy in copies:
        copy.wait()


def gate_kernel(x_ref, *refs):
    del x_ref, refs


def prefix_kernel(in_ref, out_ref, *, count, rows, self_scale, cross_scale):
    total = in_ref[0, rows:, :]
    for j in range(1, count):
        total = total + in_ref[j, rows:, :]
    state = total * cross_scale
    for j in range(count):
        out_ref[j] = state
        state = state + in_ref[j, :rows, :] * self_scale


def masked_scores(q, k, self_scale):
    length = q.shape[0]
    causal = lax.broadcasted_iota(jnp.int32, (length, length), 0) >= lax.broadcasted_iota(jnp.int32, (length, length), 1)
    return causal, halves(jnp.where(causal, dot(q, k, 1, 1), 0.0) * self_scale)


def within_kernel(q_ref, k_ref, v_ref, out_ref, *, heads, self_scale):
    for h in range(heads):
        v = v_ref[:, head(h)]
        _, (high, low) = masked_scores(q_ref[:, head(h)], k_ref[:, head(h)], self_scale)
        out_ref[:, head(h)] = dot(high, v, 1, 0) + dot(low, v, 1, 0)


def forward_kernel(q_ref, within_ref, c_ref, gain_ref, att_ref, mix_ref, *, heads):
    for h in range(heads):
        q = q_ref[:, head(h)]
        c_high, c_low = halves(c_ref[head(h), :])
        mixture = within_ref[:, head(h)] + dot(q, c_high, 1, 0) + dot(q, c_low, 1, 0)
        mix_ref[:, head(h)] = mixture
        inverse = lax.rsqrt(jnp.mean(mixture * mixture, axis=-1, keepdims=True) + 1e-06)
        att_ref[:, head(h)] = (mixture * inverse * gain_ref[h : h + 1, :]).astype(bf16)


def cotangent_kernel(place_ref, *refs, heads, rows, parts):
    blocks = refs[: len(parts)]
    w_ref, q_ref, mix_ref, gain_ref, out_ref, high_ref, low_ref = refs[len(parts) : len(parts) + 7]
    held, sems = refs[len(parts) + 7 : -1], refs[-1]
    loads = [pltpu.make_async_copy(a, b, sems.at[i]) for i, (a, b) in enumerate(zip(blocks, held))]
    for load in loads:
        load.start()
    length, width = held[0].shape[1:]
    chip, core = place_ref[0], place_ref[1]
    chips = w_ref.shape[1] // (2 * width)
    grad_normed = jnp.zeros((length, width), f32)
    for load, ref, part in zip(loads, held, parts):
        load.wait()
        for b, (steps, swapped, which) in enumerate(part):
            side = 1 - core if swapped else core
            source = lax.rem(chip + chips + (2 * side - 1) * steps, chips)
            at = 2 * source + (side if which is None else which)
            columns = pl.ds(pl.multiple_of(at * width, width), width)
            grad_normed = grad_normed + dot(ref[b], w_ref[:, columns], 1, 1)
    per = DH // rows
    gains = []
    for h in range(heads):
        mixture = mix_ref[:, head(h)]
        inverse = lax.rsqrt(jnp.mean(mixture * mixture, axis=-1, keepdims=True) + 1e-06)
        part = grad_normed[:, head(h)]
        gains.append(jnp.sum(part * (mixture * inverse), axis=0, keepdims=True))
        gained = part * gain_ref[h : h + 1, :]
        inner = jnp.mean(gained * mixture, axis=-1, keepdims=True)
        grad_mixture = inverse * gained - mixture * (inverse * inverse * inverse * inner)
        high, low = halves(grad_mixture)
        high_ref[:, head(h)] = high
        low_ref[:, head(h)] = low
        q = q_ref[:, head(h)]
        outer = dot(q, high, 0, 0) + dot(q, low, 0, 0)
        out_ref[h * per : (h + 1) * per, :rows, :] = outer.reshape(per, rows, DH)
    gain = jnp.concatenate(gains + [jnp.zeros((rows - heads, DH), f32)], axis=0)
    out_ref[:, rows:, :] = jnp.broadcast_to(gain[None], (heads * per, rows, DH))


def local_kernel(q_ref, k_ref, v_ref, c_ref, gh_ref, gl_ref, gq_ref, gk_ref, gv_ref, *, heads, self_scale):
    for h in range(heads):
        q, k, v = q_ref[:, head(h)], k_ref[:, head(h)], v_ref[:, head(h)]
        high, low = gh_ref[:, head(h)], gl_ref[:, head(h)]
        causal, (m_high, m_low) = masked_scores(q, k, self_scale)
        scores = jnp.where(causal, dot(high, v, 1, 1) + dot(low, v, 1, 1), 0.0) * self_scale
        s_high, s_low = halves(scores)
        c_high, c_low = halves(c_ref[head(h), :])
        grad_query = dot(s_high, k, 1, 0) + dot(s_low, k, 1, 0)
        grad_query = grad_query + dot(high, c_high, 1, 1) + dot(high, c_low, 1, 1) + dot(low, c_high, 1, 1)
        gq_ref[:, head(h)] = grad_query.astype(bf16)
        gk_ref[:, head(h)] = dot(s_high, q, 0, 0) + dot(s_low, q, 0, 0)
        gv_ref[:, head(h)] = dot(m_high, high, 0, 0) + dot(m_high, low, 0, 0) + dot(m_low, high, 0, 0)


def suffix_kernel(in_ref, out_ref, gain_ref, *, count, rows, heads, self_scale, cross_scale):
    gain = in_ref[0, rows:, :]
    for j in range(1, count):
        gain = gain + in_ref[j, rows:, :]
    gain_ref[...] = gain[:heads, :]
    state = jnp.zeros((rows, DH), f32)
    for j in range(count - 1, -1, -1):
        out_ref[j, :rows, :] = state * self_scale
        state = state + in_ref[j, :rows, :]
    total = state * cross_scale
    for j in range(count):
        out_ref[j, rows:, :] = total


def final_kernel(k_ref, v_ref, sk_ref, sv_ref, s_ref, gk_ref, gv_ref, out_k, out_v, out_sk, out_sv, *, heads, rows):
    per = DH // rows
    for h in range(heads):
        later = s_ref[h * per : (h + 1) * per, :rows, :].reshape(DH, DH)
        total = s_ref[h * per : (h + 1) * per, rows:, :].reshape(DH, DH)
        l_high, l_low = halves(later)
        t_high, t_low = halves(total)
        k, v, sk, sv = k_ref[:, head(h)], v_ref[:, head(h)], sk_ref[:, head(h)], sv_ref[:, head(h)]
        out_k[:, head(h)] = (gk_ref[:, head(h)] + dot(v, l_high, 1, 1) + dot(v, l_low, 1, 1)).astype(bf16)
        out_v[:, head(h)] = (gv_ref[:, head(h)] + dot(k, l_high, 1, 0) + dot(k, l_low, 1, 0)).astype(bf16)
        out_sk[:, head(h)] = (dot(sv, t_high, 1, 1) + dot(sv, t_low, 1, 1)).astype(bf16)
        out_sv[:, head(h)] = (dot(sk, t_high, 1, 0) + dot(sk, t_low, 1, 0)).astype(bf16)


WHOLE = pl.BlockSpec(memory_space=pltpu.VMEM)
SCALAR = pl.BlockSpec(memory_space=pltpu.SMEM)
ANY = pl.BlockSpec(memory_space=pl.ANY)
HBM = pl.BlockSpec(memory_space=pltpu.HBM)


MICROSECONDS = {"states": 10, "pack": 10, "within": 20, "forward": 2, "cotangent": 3, "local": 3}


def call(kernel, outs, name, ins=None, scratch=(), aliases=None, out_specs=None, **static):
    shapes = [jax.ShapeDtypeStruct(shape, dtype) for shape, dtype in outs]

    def run(*operands):
        return pl.pallas_call(
            functools.partial(kernel, **static),
            out_shape=shapes,
            in_specs=ins or [WHOLE] * len(operands),
            out_specs=out_specs or [WHOLE] * len(shapes),
            scratch_shapes=scratch,
            input_output_aliases=aliases or {},
            compiler_params=pltpu.CompilerParams(vmem_limit_bytes=12 * MIB),
            name=name,
            cost_estimate=pl.CostEstimate(flops=0, transcendentals=0, bytes_accessed=int(MICROSECONDS.get(name, 0.5) * 3.69e6)),
        )(*operands)

    return run


def pack(parts, after):
    shape = (sum(part.shape[0] for part in parts), *parts[0].shape[1:])
    return call(
        pack_kernel,
        [(shape, parts[0].dtype)],
        "pack",
        ins=[ANY] * (len(parts) + 1),
        scratch=[pltpu.SemaphoreType.DMA((len(parts),))],
    )(*parts, after)[0]


def gate(x, *after):
    outs = [(x.shape, x.dtype)]
    return call(gate_kernel, outs, "gate", ins=[ANY] * (1 + len(after)), aliases={0: 0}, out_specs=[ANY])(x, *after)[0]


def on_device(queries, keys, values, src_keys, src_values, norm_gain, out_weight, grad_out):
    length, width = queries.shape
    src_length = src_keys.shape[0]
    heads = width // DH
    count = lax.axis_size("seq")
    groups = lax.axis_size("heads")
    rows = width // count
    self_scale = 1.0 / math.sqrt(DH * length * count)
    cross_scale = 1.0 / math.sqrt(DH * src_length * count)
    gain = norm_gain.reshape(heads, DH)

    chips = groups // 2
    chip = lax.axis_index("heads") // 2
    core = lax.axis_index("heads") % 2
    place = jnp.stack([chip, core]).astype(jnp.int32)

    def along(d):
        return [(2 * y + c, 2 * ((y + (d if c == 0 else -d)) % chips) + c) for y in range(chips) for c in range(2)]

    across = lax.ppermute(grad_out[None], "heads", along(chips // 2))
    (own,) = call(
        states_kernel,
        [((count, 2 * rows, DH), f32)],
        "states",
        ins=[HBM] * 4,
        scratch=[pltpu.VMEM(x.shape, x.dtype) for x in (keys, values, src_keys, src_values)] + [pltpu.SemaphoreType.DMA((4,))],
        heads=heads,
        rows=rows,
    )(*(pltpu.with_memory_space_constraint(x, pltpu.HBM) for x in (keys, values, src_keys, src_values)))
    held = jnp.concatenate([grad_out[None], across], axis=0)
    held_next = lax.ppermute(held, "heads", along(2))
    own = lax.all_to_all(own, "seq", 0, 0)
    (before,) = call(
        prefix_kernel, [((count, rows, DH), f32)], "prefix", count=count, rows=rows, self_scale=self_scale, cross_scale=cross_scale
    )(own)
    held = jnp.concatenate([held, gate(held_next, before)], axis=0)
    got = lax.ppermute(held, "heads", along(1))
    swap = [(i, i ^ 1) for i in range(groups)]
    other_held = lax.ppermute(held, "heads", swap)
    before = lax.all_to_all(before, "seq", 0, 0).reshape(width, DH)
    (within,) = call(within_kernel, [((length, width), f32)], "within", heads=heads, self_scale=self_scale)(queries, keys, values)
    got = gate(got, before, within)
    other_got = lax.ppermute(got, "heads", swap)
    attended, mixture = call(forward_kernel, [((length, width), bf16), ((length, width), f32)], "forward", heads=heads)(
        queries, within, before, gain
    )
    blocks = [held, other_held, got, other_got]
    quad = [(0, None), (4, None), (2, None), (6, None)]
    parts = [[((d + far) % chips, swapped, None) for d, _ in quad] for far in (0, 1) for swapped in (False, True)]
    outer, g_high, g_low = call(
        cotangent_kernel,
        [((count, 2 * rows, DH), f32), ((length, width), bf16), ((length, width), bf16)],
        "cotangent",
        ins=[SCALAR] + [ANY] * len(blocks) + [WHOLE] * 4,
        scratch=[pltpu.VMEM(x.shape, x.dtype) for x in blocks] + [pltpu.SemaphoreType.DMA((len(blocks),))],
        heads=heads,
        rows=rows,
        parts=parts,
    )(place, *blocks, out_weight, queries, mixture, gain)
    outer = lax.all_to_all(outer, "seq", 0, 0)
    grad_query, grad_key, grad_value = call(
        local_kernel,
        [((length, width), bf16), ((length, width), f32), ((length, width), f32)],
        "local",
        heads=heads,
        self_scale=self_scale,
    )(queries, keys, values, before, g_high, g_low)
    later, grad_gain = call(
        suffix_kernel,
        [((count, 2 * rows, DH), f32), ((heads, DH), f32)],
        "suffix",
        count=count,
        rows=rows,
        heads=heads,
        self_scale=self_scale,
        cross_scale=cross_scale,
    )(outer)
    later = lax.all_to_all(later, "seq", 0, 0)
    grad_key, grad_value, grad_src_key, grad_src_value = call(
        final_kernel,
        [((length, width), bf16), ((length, width), bf16), ((src_length, width), bf16), ((src_length, width), bf16)],
        "final",
        heads=heads,
        rows=rows,
    )(keys, values, src_keys, src_values, later, grad_key, grad_value)
    return attended, grad_query, grad_key, grad_value, grad_src_key, grad_src_value, grad_gain.reshape(width)


def solution(mesh):
    block = P("seq", "heads")
    return jax.shard_map(
        on_device,
        mesh=mesh,
        in_specs=(block, block, block, block, block, P("heads"), P("heads", None), block),
        out_specs=(block, block, block, block, block, block, P("heads")),
        check_vma=False,
    )
```

```python
import functools
import math

import jax
import jax.numpy as jnp
from jax import lax
from jax.experimental import pallas as pl
from jax.experimental.pallas import tpu as pltpu
from jax.sharding import PartitionSpec as P

DH = 128
f32 = jnp.float32
bf16 = jnp.bfloat16
MIB = 1024 * 1024


def dot(a, b, over_a, over_b):
    return lax.dot_general(a, b, (((over_a,), (over_b,)), ((), ())), preferred_element_type=f32)


def halves(x):
    high = x.astype(bf16)
    return high, (x - high.astype(f32)).astype(bf16)


def head(h):
    return slice(h * DH, (h + 1) * DH)


def states_kernel(k_hbm, v_hbm, sk_hbm, sv_hbm, out_ref, k_ref, v_ref, sk_ref, sv_ref, sems, *, heads, rows):
    pairs = ((k_hbm, k_ref), (v_hbm, v_ref), (sk_hbm, sk_ref), (sv_hbm, sv_ref))
    loads = [pltpu.make_async_copy(a, b, sems.at[i]) for i, (a, b) in enumerate(pairs)]
    for load in loads:
        load.start()
    per = DH // rows
    for at, left, right in ((0, k_ref, v_ref), (1, sk_ref, sv_ref)):
        loads[2 * at].wait()
        loads[2 * at + 1].wait()
        for h in range(heads):
            state = dot(left[:, head(h)], right[:, head(h)], 0, 0)
            out_ref[h * per : (h + 1) * per, at * rows : (at + 1) * rows, :] = state.reshape(per, rows, DH)


def pack_kernel(*refs):
    *parts, _, out_ref, sems = refs
    copies, at = [], 0
    for i, part in enumerate(parts):
        copies.append(pltpu.make_async_copy(part, out_ref.at[at : at + part.shape[0]], sems.at[i]))
        at += part.shape[0]
    for copy in copies:
        copy.start()
    for copy in copies:
        copy.wait()


def gate_kernel(x_ref, *refs):
    del x_ref, refs


def prefix_kernel(in_ref, out_ref, *, count, rows, self_scale, cross_scale):
    total = in_ref[0, rows:, :]
    for j in range(1, count):
        total = total + in_ref[j, rows:, :]
    state = total * cross_scale
    for j in range(count):
        out_ref[j] = state
        state = state + in_ref[j, :rows, :] * self_scale


def masked_scores(q, k, self_scale):
    length = q.shape[0]
    causal = lax.broadcasted_iota(jnp.int32, (length, length), 0) >= lax.broadcasted_iota(jnp.int32, (length, length), 1)
    return causal, halves(jnp.where(causal, dot(q, k, 1, 1), 0.0) * self_scale)


def within_kernel(q_ref, k_ref, v_ref, _, out_ref, *, heads, self_scale):
    for h in range(heads):
        v = v_ref[:, head(h)]
        _, (high, low) = masked_scores(q_ref[:, head(h)], k_ref[:, head(h)], self_scale)
        out_ref[:, head(h)] = dot(high, v, 1, 0) + dot(low, v, 1, 0)


def forward_kernel(q_ref, within_ref, c_ref, gain_ref, att_ref, mix_ref, *, heads):
    for h in range(heads):
        q = q_ref[:, head(h)]
        c_high, c_low = halves(c_ref[head(h), :])
        mixture = within_ref[:, head(h)] + dot(q, c_high, 1, 0) + dot(q, c_low, 1, 0)
        mix_ref[:, head(h)] = mixture
        inverse = lax.rsqrt(jnp.mean(mixture * mixture, axis=-1, keepdims=True) + 1e-06)
        att_ref[:, head(h)] = (mixture * inverse * gain_ref[h : h + 1, :]).astype(bf16)


def cotangent_kernel(place_ref, *refs, heads, rows, parts):
    blocks = refs[: len(parts)]
    w_ref, q_ref, mix_ref, gain_ref, out_ref, high_ref, low_ref = refs[len(parts) : len(parts) + 7]
    held, sems = refs[len(parts) + 7 : -1], refs[-1]
    loads = [pltpu.make_async_copy(a, b, sems.at[i]) for i, (a, b) in enumerate(zip(blocks, held))]
    for load in loads:
        load.start()
    length, width = held[0].shape[1:]
    chip, core = place_ref[0], place_ref[1]
    chips = w_ref.shape[1] // (2 * width)
    grad_normed = jnp.zeros((length, width), f32)
    for load, ref, part in zip(loads, held, parts):
        load.wait()
        for b, (steps, swapped, which) in enumerate(part):
            side = 1 - core if swapped else core
            source = lax.rem(chip + chips + (2 * side - 1) * steps, chips)
            at = 2 * source + (side if which is None else which)
            columns = pl.ds(pl.multiple_of(at * width, width), width)
            grad_normed = grad_normed + dot(ref[b], w_ref[:, columns], 1, 1)
    per = DH // rows
    gains = []
    for h in range(heads):
        mixture = mix_ref[:, head(h)]
        inverse = lax.rsqrt(jnp.mean(mixture * mixture, axis=-1, keepdims=True) + 1e-06)
        part = grad_normed[:, head(h)]
        gains.append(jnp.sum(part * (mixture * inverse), axis=0, keepdims=True))
        gained = part * gain_ref[h : h + 1, :]
        inner = jnp.mean(gained * mixture, axis=-1, keepdims=True)
        grad_mixture = inverse * gained - mixture * (inverse * inverse * inverse * inner)
        high, low = halves(grad_mixture)
        high_ref[:, head(h)] = high
        low_ref[:, head(h)] = low
        q = q_ref[:, head(h)]
        outer = dot(q, high, 0, 0) + dot(q, low, 0, 0)
        out_ref[h * per : (h + 1) * per, :rows, :] = outer.reshape(per, rows, DH)
    gain = jnp.concatenate(gains + [jnp.zeros((rows - heads, DH), f32)], axis=0)
    out_ref[:, rows:, :] = jnp.broadcast_to(gain[None], (heads * per, rows, DH))


def local_kernel(q_ref, k_ref, v_ref, c_ref, gh_ref, gl_ref, gq_ref, gk_ref, gv_ref, *, heads, self_scale):
    for h in range(heads):
        q, k, v = q_ref[:, head(h)], k_ref[:, head(h)], v_ref[:, head(h)]
        high, low = gh_ref[:, head(h)], gl_ref[:, head(h)]
        causal, (m_high, m_low) = masked_scores(q, k, self_scale)
        scores = jnp.where(causal, dot(high, v, 1, 1) + dot(low, v, 1, 1), 0.0) * self_scale
        s_high, s_low = halves(scores)
        c_high, c_low = halves(c_ref[head(h), :])
        grad_query = dot(s_high, k, 1, 0) + dot(s_low, k, 1, 0)
        grad_query = grad_query + dot(high, c_high, 1, 1) + dot(high, c_low, 1, 1) + dot(low, c_high, 1, 1)
        gq_ref[:, head(h)] = grad_query.astype(bf16)
        gk_ref[:, head(h)] = dot(s_high, q, 0, 0) + dot(s_low, q, 0, 0)
        gv_ref[:, head(h)] = dot(m_high, high, 0, 0) + dot(m_high, low, 0, 0) + dot(m_low, high, 0, 0)


def suffix_kernel(in_ref, out_ref, gain_ref, *, count, rows, heads, self_scale, cross_scale):
    gain = in_ref[0, rows:, :]
    for j in range(1, count):
        gain = gain + in_ref[j, rows:, :]
    gain_ref[...] = gain[:heads, :]
    state = jnp.zeros((rows, DH), f32)
    for j in range(count - 1, -1, -1):
        out_ref[j, :rows, :] = state * self_scale
        state = state + in_ref[j, :rows, :]
    total = state * cross_scale
    for j in range(count):
        out_ref[j, rows:, :] = total


def final_kernel(k_ref, v_ref, sk_ref, sv_ref, s_ref, gk_ref, gv_ref, out_k, out_v, out_sk, out_sv, *, heads, rows):
    per = DH // rows
    for h in range(heads):
        later = s_ref[h * per : (h + 1) * per, :rows, :].reshape(DH, DH)
        total = s_ref[h * per : (h + 1) * per, rows:, :].reshape(DH, DH)
        l_high, l_low = halves(later)
        t_high, t_low = halves(total)
        k, v, sk, sv = k_ref[:, head(h)], v_ref[:, head(h)], sk_ref[:, head(h)], sv_ref[:, head(h)]
        out_k[:, head(h)] = (gk_ref[:, head(h)] + dot(v, l_high, 1, 1) + dot(v, l_low, 1, 1)).astype(bf16)
        out_v[:, head(h)] = (gv_ref[:, head(h)] + dot(k, l_high, 1, 0) + dot(k, l_low, 1, 0)).astype(bf16)
        out_sk[:, head(h)] = (dot(sv, t_high, 1, 1) + dot(sv, t_low, 1, 1)).astype(bf16)
        out_sv[:, head(h)] = (dot(sk, t_high, 1, 0) + dot(sk, t_low, 1, 0)).astype(bf16)


WHOLE = pl.BlockSpec(memory_space=pltpu.VMEM)
SCALAR = pl.BlockSpec(memory_space=pltpu.SMEM)
ANY = pl.BlockSpec(memory_space=pl.ANY)
HBM = pl.BlockSpec(memory_space=pltpu.HBM)


MICROSECONDS = {"states": 40, "pack": 40, "within": 40, "forward": 40, "cotangent": 3, "local": 3}


def call(kernel, outs, name, ins=None, scratch=(), aliases=None, out_specs=None, **static):
    shapes = [jax.ShapeDtypeStruct(shape, dtype) for shape, dtype in outs]

    def run(*operands):
        return pl.pallas_call(
            functools.partial(kernel, **static),
            out_shape=shapes,
            in_specs=ins or [WHOLE] * len(operands),
            out_specs=out_specs or [WHOLE] * len(shapes),
            scratch_shapes=scratch,
            input_output_aliases=aliases or {},
            compiler_params=pltpu.CompilerParams(vmem_limit_bytes=12 * MIB),
            name=name,
            cost_estimate=pl.CostEstimate(flops=int(MICROSECONDS.get(name, 0.5) * 1e9), transcendentals=0, bytes_accessed=int(MICROSECONDS.get(name, 0.5) * 3.69e6)),
        )(*operands)

    return run


def pack(parts, after):
    shape = (sum(part.shape[0] for part in parts), *parts[0].shape[1:])
    return call(
        pack_kernel,
        [(shape, parts[0].dtype)],
        "pack",
        ins=[ANY] * (len(parts) + 1),
        scratch=[pltpu.SemaphoreType.DMA((len(parts),))],
    )(*parts, after)[0]


def gate(x, *after):
    outs = [(x.shape, x.dtype)]
    return call(gate_kernel, outs, "gate", ins=[ANY] * (1 + len(after)), aliases={0: 0}, out_specs=[ANY])(x, *after)[0]


def on_device(queries, keys, values, src_keys, src_values, norm_gain, out_weight, grad_out):
    length, width = queries.shape
    src_length = src_keys.shape[0]
    heads = width // DH
    count = lax.axis_size("seq")
    groups = lax.axis_size("heads")
    rows = width // count
    self_scale = 1.0 / math.sqrt(DH * length * count)
    cross_scale = 1.0 / math.sqrt(DH * src_length * count)
    gain = norm_gain.reshape(heads, DH)

    chips = groups // 2
    chip = lax.axis_index("heads") // 2
    core = lax.axis_index("heads") % 2
    place = jnp.stack([chip, core]).astype(jnp.int32)

    def along(d):
        return [(2 * y + c, 2 * ((y + (d if c == 0 else -d)) % chips) + c) for y in range(chips) for c in range(2)]

    across = lax.ppermute(grad_out[None], "heads", along(chips // 2))
    (own,) = call(
        states_kernel,
        [((count, 2 * rows, DH), f32)],
        "states",
        ins=[HBM] * 4,
        scratch=[pltpu.VMEM(x.shape, x.dtype) for x in (keys, values, src_keys, src_values)] + [pltpu.SemaphoreType.DMA((4,))],
        heads=heads,
        rows=rows,
    )(*(pltpu.with_memory_space_constraint(x, pltpu.HBM) for x in (keys, values, src_keys, src_values)))
    held = pack([grad_out[None], across], grad_out)
    second, above, below = (lax.ppermute(held, "heads", along(d)) for d in (2, 1, -1))
    own = lax.all_to_all(own, "seq", 0, 0)
    (before,) = call(
        prefix_kernel, [((count, rows, DH), f32)], "prefix", count=count, rows=rows, self_scale=self_scale, cross_scale=cross_scale
    )(own)
    (within,) = call(
        within_kernel, [((length, width), f32)], "within", ins=[WHOLE] * 3 + [ANY], heads=heads, self_scale=self_scale
    )(queries, keys, values, before)
    second, above, below = (gate(x, within) for x in (second, above, below))
    swap = [(i, i ^ 1) for i in range(groups)]
    even = jnp.concatenate([held, second], axis=0)
    odd = jnp.concatenate([above, below], axis=0)
    other_even, other_odd = (lax.ppermute(x, "heads", swap) for x in (even, odd))
    before = lax.all_to_all(before, "seq", 0, 0).reshape(width, DH)
    attended, mixture = call(forward_kernel, [((length, width), bf16), ((length, width), f32)], "forward", heads=heads)(
        queries, within, before, gain
    )
    blocks = [even, odd, other_even, other_odd]
    parts = [[(d, swapped, None) for d in steps] for swapped in (False, True) for steps in ((0, 4, 2, 6), (1, 5, 7, 3))]
    outer, g_high, g_low = call(
        cotangent_kernel,
        [((count, 2 * rows, DH), f32), ((length, width), bf16), ((length, width), bf16)],
        "cotangent",
        ins=[SCALAR] + [ANY] * len(blocks) + [WHOLE] * 4,
        scratch=[pltpu.VMEM(x.shape, x.dtype) for x in blocks] + [pltpu.SemaphoreType.DMA((len(blocks),))],
        heads=heads,
        rows=rows,
        parts=parts,
    )(place, *blocks, out_weight, queries, mixture, gain)
    outer = lax.all_to_all(outer, "seq", 0, 0)
    grad_query, grad_key, grad_value = call(
        local_kernel,
        [((length, width), bf16), ((length, width), f32), ((length, width), f32)],
        "local",
        heads=heads,
        self_scale=self_scale,
    )(queries, keys, values, before, g_high, g_low)
    later, grad_gain = call(
        suffix_kernel,
        [((count, 2 * rows, DH), f32), ((heads, DH), f32)],
        "suffix",
        count=count,
        rows=rows,
        heads=heads,
        self_scale=self_scale,
        cross_scale=cross_scale,
    )(outer)
    later = lax.all_to_all(later, "seq", 0, 0)
    grad_key, grad_value, grad_src_key, grad_src_value = call(
        final_kernel,
        [((length, width), bf16), ((length, width), bf16), ((src_length, width), bf16), ((src_length, width), bf16)],
        "final",
        heads=heads,
        rows=rows,
    )(keys, values, src_keys, src_values, later, grad_key, grad_value)
    return attended, grad_query, grad_key, grad_value, grad_src_key, grad_src_value, grad_gain.reshape(width)


def solution(mesh):
    block = P("seq", "heads")
    return jax.shard_map(
        on_device,
        mesh=mesh,
        in_specs=(block, block, block, block, block, P("heads"), P("heads", None), block),
        out_specs=(block, block, block, block, block, block, P("heads")),
        check_vma=False,
    )
```

```python
import functools
import math

import jax
import jax.numpy as jnp
from jax import lax
from jax.experimental import pallas as pl
from jax.experimental.pallas import tpu as pltpu
from jax.sharding import PartitionSpec as P

DH = 128
f32 = jnp.float32
bf16 = jnp.bfloat16
MIB = 1024 * 1024


def dot(a, b, over_a, over_b):
    return lax.dot_general(a, b, (((over_a,), (over_b,)), ((), ())), preferred_element_type=f32)


def halves(x):
    high = x.astype(bf16)
    return high, (x - high.astype(f32)).astype(bf16)


def head(h):
    return slice(h * DH, (h + 1) * DH)


def states_kernel(k_hbm, v_hbm, sk_hbm, sv_hbm, out_ref, k_ref, v_ref, sk_ref, sv_ref, sems, *, heads, rows):
    pairs = ((k_hbm, k_ref), (v_hbm, v_ref), (sk_hbm, sk_ref), (sv_hbm, sv_ref))
    loads = [pltpu.make_async_copy(a, b, sems.at[i]) for i, (a, b) in enumerate(pairs)]
    for load in loads:
        load.start()
    per = DH // rows
    for at, left, right in ((0, k_ref, v_ref), (1, sk_ref, sv_ref)):
        loads[2 * at].wait()
        loads[2 * at + 1].wait()
        for h in range(heads):
            state = dot(left[:, head(h)], right[:, head(h)], 0, 0)
            out_ref[h * per : (h + 1) * per, at * rows : (at + 1) * rows, :] = state.reshape(per, rows, DH)


def pack_kernel(*refs):
    *parts, _, out_ref, sems = refs
    copies, at = [], 0
    for i, part in enumerate(parts):
        copies.append(pltpu.make_async_copy(part, out_ref.at[at : at + part.shape[0]], sems.at[i]))
        at += part.shape[0]
    for copy in copies:
        copy.start()
    for copy in copies:
        copy.wait()


def gate_kernel(x_ref, *refs):
    del x_ref, refs


def prefix_kernel(in_ref, out_ref, *, count, rows, self_scale, cross_scale):
    total = in_ref[0, rows:, :]
    for j in range(1, count):
        total = total + in_ref[j, rows:, :]
    state = total * cross_scale
    for j in range(count):
        out_ref[j] = state
        state = state + in_ref[j, :rows, :] * self_scale


def masked_scores(q, k, self_scale):
    length = q.shape[0]
    causal = lax.broadcasted_iota(jnp.int32, (length, length), 0) >= lax.broadcasted_iota(jnp.int32, (length, length), 1)
    return causal, halves(jnp.where(causal, dot(q, k, 1, 1), 0.0) * self_scale)


def within_kernel(q_ref, k_ref, v_ref, _, out_ref, *, heads, self_scale):
    for h in range(heads):
        v = v_ref[:, head(h)]
        _, (high, low) = masked_scores(q_ref[:, head(h)], k_ref[:, head(h)], self_scale)
        out_ref[:, head(h)] = dot(high, v, 1, 0) + dot(low, v, 1, 0)


def forward_kernel(q_ref, within_ref, c_ref, mix_ref, *, heads):
    for h in range(heads):
        q = q_ref[:, head(h)]
        c_high, c_low = halves(c_ref[head(h), :])
        mixture = within_ref[:, head(h)] + dot(q, c_high, 1, 0) + dot(q, c_low, 1, 0)
        mix_ref[:, head(h)] = mixture


def cotangent_kernel(place_ref, *refs, heads, rows, parts):
    held = refs[: len(parts)]
    w_ref, q_ref, mix_ref, gain_ref, out_ref, high_ref, low_ref = refs[len(parts) :]
    length, width = held[0].shape[1:]
    chip, core = place_ref[0], place_ref[1]
    chips = w_ref.shape[1] // (2 * width)
    grad_normed = jnp.zeros((length, width), f32)
    for ref, part in zip(held, parts):
        for b, (steps, swapped, which) in enumerate(part):
            side = 1 - core if swapped else core
            source = lax.rem(chip + chips + (2 * side - 1) * steps, chips)
            at = 2 * source + (side if which is None else which)
            columns = pl.ds(pl.multiple_of(at * width, width), width)
            grad_normed = grad_normed + dot(ref[b], w_ref[:, columns], 1, 1)
    per = DH // rows
    gains = []
    for h in range(heads):
        mixture = mix_ref[:, head(h)]
        inverse = lax.rsqrt(jnp.mean(mixture * mixture, axis=-1, keepdims=True) + 1e-06)
        part = grad_normed[:, head(h)]
        gains.append(jnp.sum(part * (mixture * inverse), axis=0, keepdims=True))
        gained = part * gain_ref[h : h + 1, :]
        inner = jnp.mean(gained * mixture, axis=-1, keepdims=True)
        grad_mixture = inverse * gained - mixture * (inverse * inverse * inverse * inner)
        high, low = halves(grad_mixture)
        high_ref[:, head(h)] = high
        low_ref[:, head(h)] = low
        q = q_ref[:, head(h)]
        outer = dot(q, high, 0, 0) + dot(q, low, 0, 0)
        for at in range(0, DH, heads):
            out_ref[h * per + at // rows, at % rows // heads] = outer[at : at + heads, :]
    gain = jnp.concatenate(gains, axis=0)
    out_ref[:, rows // heads] = jnp.broadcast_to(gain[None], (heads * per, heads, DH))


def local_kernel(
    q_ref, k_ref, v_ref, c_ref, mix_ref, gain_ref, gh_ref, gl_ref, att_ref, gq_ref, gk_ref, gv_ref, *, heads, self_scale
):
    for h in range(heads):
        mixture = mix_ref[:, head(h)]
        inverse = lax.rsqrt(jnp.mean(mixture * mixture, axis=-1, keepdims=True) + 1e-06)
        att_ref[:, head(h)] = (mixture * inverse * gain_ref[h : h + 1, :]).astype(bf16)
        q, k, v = q_ref[:, head(h)], k_ref[:, head(h)], v_ref[:, head(h)]
        high, low = gh_ref[:, head(h)], gl_ref[:, head(h)]
        causal, (m_high, m_low) = masked_scores(q, k, self_scale)
        scores = jnp.where(causal, dot(high, v, 1, 1) + dot(low, v, 1, 1), 0.0) * self_scale
        s_high, s_low = halves(scores)
        c_high, c_low = halves(c_ref[head(h), :])
        grad_query = dot(s_high, k, 1, 0) + dot(s_low, k, 1, 0)
        grad_query = grad_query + dot(high, c_high, 1, 1) + dot(high, c_low, 1, 1) + dot(low, c_high, 1, 1)
        gq_ref[:, head(h)] = grad_query.astype(bf16)
        gk_ref[:, head(h)] = dot(s_high, q, 0, 0) + dot(s_low, q, 0, 0)
        gv_ref[:, head(h)] = dot(m_high, high, 0, 0) + dot(m_high, low, 0, 0) + dot(m_low, high, 0, 0)


def suffix_kernel(in_ref, out_ref, gain_ref, *, count, rows, heads, self_scale, cross_scale):
    tiles = rows // heads
    gain = in_ref[0, tiles]
    for j in range(1, count):
        gain = gain + in_ref[j, tiles]
    gain_ref[...] = gain
    for tile in range(tiles):
        at = tile * heads
        state = jnp.zeros((heads, DH), f32)
        for j in range(count):
            out_ref[j, at : at + heads, :] = state * self_scale
            state = state + in_ref[j, tile]
        total = state * cross_scale
        for j in range(count):
            out_ref[j, rows + at : rows + at + heads, :] = total


def final_kernel(k_ref, v_ref, sk_ref, sv_ref, s_ref, gk_ref, gv_ref, out_k, out_v, out_sk, out_sv, *, heads, rows):
    per = DH // rows
    for h in range(heads):
        later = s_ref[h * per : (h + 1) * per, :rows, :].reshape(DH, DH)
        total = s_ref[h * per : (h + 1) * per, rows:, :].reshape(DH, DH)
        l_high, l_low = halves(later)
        t_high, t_low = halves(total)
        k, v, sk, sv = k_ref[:, head(h)], v_ref[:, head(h)], sk_ref[:, head(h)], sv_ref[:, head(h)]
        out_k[:, head(h)] = (gk_ref[:, head(h)] + dot(v, l_high, 1, 1) + dot(v, l_low, 1, 1)).astype(bf16)
        out_v[:, head(h)] = (gv_ref[:, head(h)] + dot(k, l_high, 1, 0) + dot(k, l_low, 1, 0)).astype(bf16)
        out_sk[:, head(h)] = (dot(sv, t_high, 1, 1) + dot(sv, t_low, 1, 1)).astype(bf16)
        out_sv[:, head(h)] = (dot(sk, t_high, 1, 0) + dot(sk, t_low, 1, 0)).astype(bf16)


WHOLE = pl.BlockSpec(memory_space=pltpu.VMEM)
SCALAR = pl.BlockSpec(memory_space=pltpu.SMEM)
ANY = pl.BlockSpec(memory_space=pl.ANY)
HBM = pl.BlockSpec(memory_space=pltpu.HBM)


MICROSECONDS = {"states": 40, "pack": 40, "within": 40, "forward": 40, "cotangent": 3, "local": 3}


def call(kernel, outs, name, ins=None, scratch=(), aliases=None, out_specs=None, **static):
    shapes = [jax.ShapeDtypeStruct(shape, dtype) for shape, dtype in outs]

    def run(*operands):
        return pl.pallas_call(
            functools.partial(kernel, **static),
            out_shape=shapes,
            in_specs=ins or [WHOLE] * len(operands),
            out_specs=out_specs or [WHOLE] * len(shapes),
            scratch_shapes=scratch,
            input_output_aliases=aliases or {},
            compiler_params=pltpu.CompilerParams(vmem_limit_bytes=12 * MIB),
            name=name,
            cost_estimate=pl.CostEstimate(flops=int(MICROSECONDS.get(name, 0.5) * 1e9), transcendentals=0, bytes_accessed=int(MICROSECONDS.get(name, 0.5) * 3.69e6)),
        )(*operands)

    return run


def pack(parts, after):
    shape = (sum(part.shape[0] for part in parts), *parts[0].shape[1:])
    return call(
        pack_kernel,
        [(shape, parts[0].dtype)],
        "pack",
        ins=[ANY] * (len(parts) + 1),
        scratch=[pltpu.SemaphoreType.DMA((len(parts),))],
    )(*parts, after)[0]


def gate(x, *after):
    outs = [(x.shape, x.dtype)]
    return call(gate_kernel, outs, "gate", ins=[ANY] * (1 + len(after)), aliases={0: 0}, out_specs=[ANY])(x, *after)[0]


def on_device(queries, keys, values, src_keys, src_values, norm_gain, out_weight, grad_out):
    length, width = queries.shape
    src_length = src_keys.shape[0]
    heads = width // DH
    count = lax.axis_size("seq")
    groups = lax.axis_size("heads")
    rows = width // count
    self_scale = 1.0 / math.sqrt(DH * length * count)
    cross_scale = 1.0 / math.sqrt(DH * src_length * count)
    gain = norm_gain.reshape(heads, DH)
    backwards = [list(range(count - 1, -1, -1))]

    chips = groups // 2
    chip = lax.axis_index("heads") // 2
    core = lax.axis_index("heads") % 2
    place = jnp.stack([chip, core]).astype(jnp.int32)

    def along(d):
        return [(2 * y + c, 2 * ((y + (d if c == 0 else -d)) % chips) + c) for y in range(chips) for c in range(2)]

    across = lax.ppermute(grad_out[None], "heads", along(4))
    (own,) = call(
        states_kernel,
        [((count, 2 * rows, DH), f32)],
        "states",
        ins=[HBM] * 4,
        scratch=[pltpu.VMEM(x.shape, x.dtype) for x in (keys, values, src_keys, src_values)] + [pltpu.SemaphoreType.DMA((4,))],
        heads=heads,
        rows=rows,
    )(*(pltpu.with_memory_space_constraint(x, pltpu.HBM) for x in (keys, values, src_keys, src_values)))
    held = pack([grad_out[None], across], grad_out)
    second, above, below = (lax.ppermute(held, "heads", along(d)) for d in (2, 1, -1))
    own = lax.all_to_all(own, "seq", 0, 0)
    (before,) = call(
        prefix_kernel, [((count, rows, DH), f32)], "prefix", count=count, rows=rows, self_scale=self_scale, cross_scale=cross_scale
    )(own)
    (within,) = call(
        within_kernel, [((length, width), f32)], "within", ins=[WHOLE] * 3 + [ANY], heads=heads, self_scale=self_scale
    )(queries, keys, values, before)
    second, above, below = (gate(x, within) for x in (second, above, below))
    whole = jnp.concatenate([held, second, above, below], axis=0)
    other = lax.ppermute(whole, "heads", [(i, i ^ 1) for i in range(groups)])
    before = lax.all_to_all(before, "seq", 0, 0).reshape(width, DH)
    (mixture,) = call(forward_kernel, [((length, width), f32)], "forward", heads=heads)(queries, within, before)
    blocks = [whole, other]
    parts = [[(d, swapped, None) for d in steps] for swapped in (False, True) for steps in ((0, 4, 2, 6, 1, 5, 7, 3),)]
    outer, g_high, g_low = call(
        cotangent_kernel,
        [((count, rows // heads + 1, heads, DH), f32), ((length, width), bf16), ((length, width), bf16)],
        "cotangent",
        ins=[SCALAR] + [WHOLE] * (len(blocks) + 4),
        heads=heads,
        rows=rows,
        parts=parts,
    )(place, *blocks, out_weight, queries, mixture, gain)
    outer = lax.all_to_all(outer, "seq", 0, 0, axis_index_groups=backwards)
    attended, grad_query, grad_key, grad_value = call(
        local_kernel,
        [((length, width), bf16), ((length, width), bf16), ((length, width), f32), ((length, width), f32)],
        "local",
        heads=heads,
        self_scale=self_scale,
    )(queries, keys, values, before, mixture, gain, g_high, g_low)
    later, grad_gain = call(
        suffix_kernel,
        [((count, 2 * rows, DH), f32), ((heads, DH), f32)],
        "suffix",
        count=count,
        rows=rows,
        heads=heads,
        self_scale=self_scale,
        cross_scale=cross_scale,
    )(outer)
    later = lax.all_to_all(later, "seq", 0, 0, axis_index_groups=backwards)
    grad_key, grad_value, grad_src_key, grad_src_value = call(
        final_kernel,
        [((length, width), bf16), ((length, width), bf16), ((src_length, width), bf16), ((src_length, width), bf16)],
        "final",
        heads=heads,
        rows=rows,
    )(keys, values, src_keys, src_values, later, grad_key, grad_value)
    return attended, grad_query, grad_key, grad_value, grad_src_key, grad_src_value, grad_gain.reshape(width)


def solution(mesh):
    block = P("seq", "heads")
    return jax.shard_map(
        on_device,
        mesh=mesh,
        in_specs=(block, block, block, block, block, P("heads"), P("heads", None), block),
        out_specs=(block, block, block, block, block, block, P("heads")),
        check_vma=False,
    )
```

```python
import functools
import math

import jax
import jax.numpy as jnp
from jax import lax
from jax.experimental import pallas as pl
from jax.experimental.pallas import tpu as pltpu
from jax.sharding import PartitionSpec as P

DH = 128
f32 = jnp.float32
bf16 = jnp.bfloat16
MIB = 1024 * 1024


def dot(a, b, over_a, over_b):
    return lax.dot_general(a, b, (((over_a,), (over_b,)), ((), ())), preferred_element_type=f32)


def halves(x):
    high = x.astype(bf16)
    return high, (x - high.astype(f32)).astype(bf16)


def beside(a, b):
    return jnp.concatenate([a, b], axis=1)


def head(h):
    return slice(h * DH, (h + 1) * DH)


def states_kernel(k_hbm, v_hbm, sk_hbm, sv_hbm, out_ref, k_ref, v_ref, sk_ref, sv_ref, sems, *, heads, rows):
    pairs = ((k_hbm, k_ref), (v_hbm, v_ref), (sk_hbm, sk_ref), (sv_hbm, sv_ref))
    loads = [pltpu.make_async_copy(a, b, sems.at[i]) for i, (a, b) in enumerate(pairs)]
    for load in loads:
        load.start()
    per = DH // rows
    for at, left, right in ((0, k_ref, v_ref), (1, sk_ref, sv_ref)):
        loads[2 * at].wait()
        loads[2 * at + 1].wait()
        for h in range(heads):
            state = dot(left[:, head(h)], right[:, head(h)], 0, 0)
            out_ref[h * per : (h + 1) * per, at * rows : (at + 1) * rows, :] = state.reshape(per, rows, DH)


def pack_kernel(*refs):
    *parts, _, out_ref, sems = refs
    copies, at = [], 0
    for i, part in enumerate(parts):
        copies.append(pltpu.make_async_copy(part, out_ref.at[at : at + part.shape[0]], sems.at[i]))
        at += part.shape[0]
    for copy in copies:
        copy.start()
    for copy in copies:
        copy.wait()


def gate_kernel(x_ref, *refs):
    del x_ref, refs


def prefix_kernel(in_ref, out_ref, *, count, rows, self_scale, cross_scale):
    total = in_ref[0, rows:, :]
    for j in range(1, count):
        total = total + in_ref[j, rows:, :]
    state = total * cross_scale
    for j in range(count):
        out_ref[j] = state
        state = state + in_ref[j, :rows, :] * self_scale


def masked_scores(q, k, self_scale):
    length = q.shape[0]
    causal = lax.broadcasted_iota(jnp.int32, (length, length), 0) >= lax.broadcasted_iota(jnp.int32, (length, length), 1)
    return causal, halves(jnp.where(causal, dot(q, k, 1, 1), 0.0) * self_scale)


def within_kernel(q_ref, k_ref, v_ref, _, out_ref, *, heads, self_scale):
    for h in range(heads):
        v = v_ref[:, head(h)]
        _, (high, low) = masked_scores(q_ref[:, head(h)], k_ref[:, head(h)], self_scale)
        out_ref[:, head(h)] = dot(high, v, 1, 0) + dot(low, v, 1, 0)


def forward_kernel(q_ref, within_ref, c_ref, mix_ref, *, heads):
    for h in range(heads):
        q = q_ref[:, head(h)]
        c_high, c_low = halves(c_ref[head(h), :])
        mixture = within_ref[:, head(h)] + dot(beside(q, q), jnp.concatenate([c_high, c_low], axis=0), 1, 0)
        mix_ref[:, head(h)] = mixture


def cotangent_kernel(place_ref, *refs, heads, rows, parts):
    held = refs[: len(parts)]
    w_ref, q_ref, mix_ref, gain_ref, out_ref, high_ref, low_ref = refs[len(parts) :]
    length, width = held[0].shape[1:]
    chip, core = place_ref[0], place_ref[1]
    chips = w_ref.shape[1] // (2 * width)
    grad_normed = jnp.zeros((length, width), f32)
    for ref, part in zip(held, parts):
        for b, (steps, swapped, which) in enumerate(part):
            side = 1 - core if swapped else core
            source = lax.rem(chip + chips + (2 * side - 1) * steps, chips)
            at = 2 * source + (side if which is None else which)
            columns = pl.ds(pl.multiple_of(at * width, width), width)
            grad_normed = grad_normed + dot(ref[b], w_ref[:, columns], 1, 1)
    per = DH // rows
    gains = []
    for h in range(heads):
        mixture = mix_ref[:, head(h)]
        inverse = lax.rsqrt(jnp.mean(mixture * mixture, axis=-1, keepdims=True) + 1e-06)
        part = grad_normed[:, head(h)]
        gains.append(jnp.sum(part * (mixture * inverse), axis=0, keepdims=True))
        gained = part * gain_ref[h : h + 1, :]
        inner = jnp.mean(gained * mixture, axis=-1, keepdims=True)
        grad_mixture = inverse * gained - mixture * (inverse * inverse * inverse * inner)
        high, low = halves(grad_mixture)
        high_ref[:, head(h)] = high
        low_ref[:, head(h)] = low
        q = q_ref[:, head(h)]
        outer = dot(q, beside(high, low), 0, 0)
        outer = outer[:, :DH] + outer[:, DH:]
        for at in range(0, DH, heads):
            out_ref[h * per + at // rows, at % rows // heads] = outer[at : at + heads, :]
    gain = jnp.concatenate(gains, axis=0)
    out_ref[:, rows // heads] = jnp.broadcast_to(gain[None], (heads * per, heads, DH))


def local_kernel(
    q_ref, k_ref, v_ref, c_ref, mix_ref, gain_ref, gh_ref, gl_ref, att_ref, gq_ref, gk_ref, gv_ref, *, heads, self_scale
):
    for h in range(heads):
        mixture = mix_ref[:, head(h)]
        inverse = lax.rsqrt(jnp.mean(mixture * mixture, axis=-1, keepdims=True) + 1e-06)
        att_ref[:, head(h)] = (mixture * inverse * gain_ref[h : h + 1, :]).astype(bf16)
        q, k, v = q_ref[:, head(h)], k_ref[:, head(h)], v_ref[:, head(h)]
        high, low = gh_ref[:, head(h)], gl_ref[:, head(h)]
        causal, (m_high, m_low) = masked_scores(q, k, self_scale)
        scores = jnp.where(causal, dot(high, v, 1, 1) + dot(low, v, 1, 1), 0.0) * self_scale
        s_high, s_low = halves(scores)
        c_high, c_low = halves(c_ref[head(h), :])
        grad_query = dot(s_high, k, 1, 0) + dot(s_low, k, 1, 0)
        grad_query = grad_query + dot(high, c_high, 1, 1) + dot(high, c_low, 1, 1) + dot(low, c_high, 1, 1)
        gq_ref[:, head(h)] = grad_query.astype(bf16)
        gk_ref[:, head(h)] = dot(s_high, q, 0, 0) + dot(s_low, q, 0, 0)
        gv_ref[:, head(h)] = dot(m_high, high, 0, 0) + dot(m_high, low, 0, 0) + dot(m_low, high, 0, 0)


def suffix_kernel(in_ref, out_ref, gain_ref, *, count, rows, heads, self_scale, cross_scale):
    tiles = rows // heads
    gain = in_ref[0, tiles]
    for j in range(1, count):
        gain = gain + in_ref[j, tiles]
    gain_ref[...] = gain
    for tile in range(tiles):
        at = tile * heads
        state = jnp.zeros((heads, DH), f32)
        for j in range(count):
            out_ref[j, at : at + heads, :] = state * self_scale
            state = state + in_ref[j, tile]
        total = state * cross_scale
        for j in range(count):
            out_ref[j, rows + at : rows + at + heads, :] = total


def final_kernel(k_ref, v_ref, sk_ref, sv_ref, s_ref, gk_ref, gv_ref, out_k, out_v, out_sk, out_sv, *, heads, rows):
    per = DH // rows
    for h in range(heads):
        later = s_ref[h * per : (h + 1) * per, :rows, :].reshape(DH, DH)
        total = s_ref[h * per : (h + 1) * per, rows:, :].reshape(DH, DH)
        l_high, l_low = halves(later)
        t_high, t_low = halves(total)
        k, v, sk, sv = k_ref[:, head(h)], v_ref[:, head(h)], sk_ref[:, head(h)], sv_ref[:, head(h)]
        out_k[:, head(h)] = (gk_ref[:, head(h)] + dot(beside(v, v), beside(l_high, l_low), 1, 1)).astype(bf16)
        out_v[:, head(h)] = (gv_ref[:, head(h)] + dot(beside(k, k), jnp.concatenate([l_high, l_low], axis=0), 1, 0)).astype(bf16)
        out_sk[:, head(h)] = (dot(beside(sv, sv), beside(t_high, t_low), 1, 1)).astype(bf16)
        out_sv[:, head(h)] = (dot(beside(sk, sk), jnp.concatenate([t_high, t_low], axis=0), 1, 0)).astype(bf16)


WHOLE = pl.BlockSpec(memory_space=pltpu.VMEM)
SCALAR = pl.BlockSpec(memory_space=pltpu.SMEM)
ANY = pl.BlockSpec(memory_space=pl.ANY)
HBM = pl.BlockSpec(memory_space=pltpu.HBM)


MICROSECONDS = {"states": 40, "pack": 40, "within": 40, "forward": 40, "cotangent": 3, "local": 3}


def call(kernel, outs, name, ins=None, scratch=(), aliases=None, out_specs=None, **static):
    shapes = [jax.ShapeDtypeStruct(shape, dtype) for shape, dtype in outs]

    def run(*operands):
        return pl.pallas_call(
            functools.partial(kernel, **static),
            out_shape=shapes,
            in_specs=ins or [WHOLE] * len(operands),
            out_specs=out_specs or [WHOLE] * len(shapes),
            scratch_shapes=scratch,
            input_output_aliases=aliases or {},
            compiler_params=pltpu.CompilerParams(vmem_limit_bytes=12 * MIB),
            name=name,
            cost_estimate=pl.CostEstimate(flops=int(MICROSECONDS.get(name, 0.5) * 1e9), transcendentals=0, bytes_accessed=int(MICROSECONDS.get(name, 0.5) * 3.69e6)),
        )(*operands)

    return run


def pack(parts, after):
    shape = (sum(part.shape[0] for part in parts), *parts[0].shape[1:])
    return call(
        pack_kernel,
        [(shape, parts[0].dtype)],
        "pack",
        ins=[ANY] * (len(parts) + 1),
        scratch=[pltpu.SemaphoreType.DMA((len(parts),))],
    )(*parts, after)[0]


def gate(x, *after):
    outs = [(x.shape, x.dtype)]
    return call(gate_kernel, outs, "gate", ins=[ANY] * (1 + len(after)), aliases={0: 0}, out_specs=[ANY])(x, *after)[0]


def on_device(queries, keys, values, src_keys, src_values, norm_gain, out_weight, grad_out):
    length, width = queries.shape
    src_length = src_keys.shape[0]
    heads = width // DH
    count = lax.axis_size("seq")
    groups = lax.axis_size("heads")
    rows = width // count
    self_scale = 1.0 / math.sqrt(DH * length * count)
    cross_scale = 1.0 / math.sqrt(DH * src_length * count)
    gain = norm_gain.reshape(heads, DH)
    backwards = [list(range(count - 1, -1, -1))]

    chips = groups // 2
    chip = lax.axis_index("heads") // 2
    core = lax.axis_index("heads") % 2
    place = jnp.stack([chip, core]).astype(jnp.int32)

    def along(d):
        return [(2 * y + c, 2 * ((y + (d if c == 0 else -d)) % chips) + c) for y in range(chips) for c in range(2)]

    across = lax.ppermute(grad_out[None], "heads", along(4))
    (own,) = call(
        states_kernel,
        [((count, 2 * rows, DH), f32)],
        "states",
        ins=[HBM] * 4,
        scratch=[pltpu.VMEM(x.shape, x.dtype) for x in (keys, values, src_keys, src_values)] + [pltpu.SemaphoreType.DMA((4,))],
        heads=heads,
        rows=rows,
    )(*(pltpu.with_memory_space_constraint(x, pltpu.HBM) for x in (keys, values, src_keys, src_values)))
    held = pack([grad_out[None], across], grad_out)
    second, above, below = (lax.ppermute(held, "heads", along(d)) for d in (2, 1, -1))
    own = lax.all_to_all(own, "seq", 0, 0)
    (before,) = call(
        prefix_kernel, [((count, rows, DH), f32)], "prefix", count=count, rows=rows, self_scale=self_scale, cross_scale=cross_scale
    )(own)
    (within,) = call(
        within_kernel, [((length, width), f32)], "within", ins=[WHOLE] * 3 + [ANY], heads=heads, self_scale=self_scale
    )(queries, keys, values, before)
    second, above, below = (gate(x, within) for x in (second, above, below))
    whole = jnp.concatenate([held, second, above, below], axis=0)
    other = lax.ppermute(whole, "heads", [(i, i ^ 1) for i in range(groups)])
    before = lax.all_to_all(before, "seq", 0, 0).reshape(width, DH)
    (mixture,) = call(forward_kernel, [((length, width), f32)], "forward", heads=heads)(queries, within, before)
    blocks = [whole, other]
    parts = [[(d, swapped, None) for d in steps] for swapped in (False, True) for steps in ((0, 4, 2, 6, 1, 5, 7, 3),)]
    outer, g_high, g_low = call(
        cotangent_kernel,
        [((count, rows // heads + 1, heads, DH), f32), ((length, width), bf16), ((length, width), bf16)],
        "cotangent",
        ins=[SCALAR] + [WHOLE] * (len(blocks) + 4),
        heads=heads,
        rows=rows,
        parts=parts,
    )(place, *blocks, out_weight, queries, mixture, gain)
    outer = lax.all_to_all(outer, "seq", 0, 0, axis_index_groups=backwards)
    attended, grad_query, grad_key, grad_value = call(
        local_kernel,
        [((length, width), bf16), ((length, width), bf16), ((length, width), f32), ((length, width), f32)],
        "local",
        heads=heads,
        self_scale=self_scale,
    )(queries, keys, values, before, mixture, gain, g_high, g_low)
    later, grad_gain = call(
        suffix_kernel,
        [((count, 2 * rows, DH), f32), ((heads, DH), f32)],
        "suffix",
        count=count,
        rows=rows,
        heads=heads,
        self_scale=self_scale,
        cross_scale=cross_scale,
    )(outer)
    later = lax.all_to_all(later, "seq", 0, 0, axis_index_groups=backwards)
    grad_key, grad_value, grad_src_key, grad_src_value = call(
        final_kernel,
        [((length, width), bf16), ((length, width), bf16), ((src_length, width), bf16), ((src_length, width), bf16)],
        "final",
        heads=heads,
        rows=rows,
    )(keys, values, src_keys, src_values, later, grad_key, grad_value)
    return attended, grad_query, grad_key, grad_value, grad_src_key, grad_src_value, grad_gain.reshape(width)


def solution(mesh):
    block = P("seq", "heads")
    return jax.shard_map(
        on_device,
        mesh=mesh,
        in_specs=(block, block, block, block, block, P("heads"), P("heads", None), block),
        out_specs=(block, block, block, block, block, block, P("heads")),
        check_vma=False,
    )
```

```python
import functools
import math

import jax
import jax.numpy as jnp
from jax import lax
from jax.experimental import pallas as pl
from jax.experimental.pallas import tpu as pltpu
from jax.sharding import PartitionSpec as P

DH = 128
f32 = jnp.float32
bf16 = jnp.bfloat16
MIB = 1024 * 1024


def dot(a, b, over_a, over_b):
    return lax.dot_general(a, b, (((over_a,), (over_b,)), ((), ())), preferred_element_type=f32)


def halves(x):
    high = x.astype(bf16)
    return high, (x - high.astype(f32)).astype(bf16)


def beside(a, b):
    return jnp.concatenate([a, b], axis=1)


def head(h):
    return slice(h * DH, (h + 1) * DH)


def states_kernel(k_hbm, v_hbm, sk_hbm, sv_hbm, out_ref, k_ref, v_ref, sk_ref, sv_ref, sems, *, heads, rows):
    pairs = ((k_hbm, k_ref), (v_hbm, v_ref), (sk_hbm, sk_ref), (sv_hbm, sv_ref))
    loads = [pltpu.make_async_copy(a, b, sems.at[i]) for i, (a, b) in enumerate(pairs)]
    for load in loads:
        load.start()
    per = DH // rows
    for at, left, right in ((0, k_ref, v_ref), (1, sk_ref, sv_ref)):
        loads[2 * at].wait()
        loads[2 * at + 1].wait()
        for h in range(heads):
            state = dot(left[:, head(h)], right[:, head(h)], 0, 0)
            out_ref[h * per : (h + 1) * per, at * rows : (at + 1) * rows, :] = state.reshape(per, rows, DH)


def pack_kernel(*refs):
    *parts, _, out_ref, sems = refs
    copies, at = [], 0
    for i, part in enumerate(parts):
        copies.append(pltpu.make_async_copy(part, out_ref.at[at : at + part.shape[0]], sems.at[i]))
        at += part.shape[0]
    for copy in copies:
        copy.start()
    for copy in copies:
        copy.wait()


def gate_kernel(x_ref, *refs):
    del x_ref, refs


def prefix_kernel(in_ref, out_ref, *, count, rows, self_scale, cross_scale):
    total = in_ref[0, rows:, :]
    for j in range(1, count):
        total = total + in_ref[j, rows:, :]
    state = total * cross_scale
    for j in range(count):
        out_ref[j] = state
        state = state + in_ref[j, :rows, :] * self_scale


def masked_scores(q, k, self_scale):
    length = q.shape[0]
    causal = lax.broadcasted_iota(jnp.int32, (length, length), 0) >= lax.broadcasted_iota(jnp.int32, (length, length), 1)
    return causal, halves(jnp.where(causal, dot(q, k, 1, 1), 0.0) * self_scale)


def within_kernel(q_ref, k_ref, v_ref, _, out_ref, *, heads, self_scale):
    for h in range(heads):
        v = v_ref[:, head(h)]
        _, (high, low) = masked_scores(q_ref[:, head(h)], k_ref[:, head(h)], self_scale)
        out_ref[:, head(h)] = dot(high, v, 1, 0) + dot(low, v, 1, 0)


def narrow_kernel(c_ref, high_ref, low_ref):
    high_ref[...], low_ref[...] = halves(c_ref[...])


def cotangent_kernel(place_ref, *refs, heads, rows, parts):
    held = refs[: len(parts)]
    w_hbm, gain_hbm, q_ref, within_ref, ch_ref, cl_ref, out_ref, high_ref, low_ref, mix_ref, w_ref, gain_ref, sems = refs[len(parts) :]
    pieces = sems.shape[0] - 1
    height = w_ref.shape[0] // pieces
    loads = [pltpu.make_async_copy(gain_hbm, gain_ref, sems.at[pieces])]
    for i in range(pieces):
        piece = slice(i * height, (i + 1) * height)
        loads.append(pltpu.make_async_copy(w_hbm.at[piece], w_ref.at[piece], sems.at[i]))
    for load in loads:
        load.start()
    for h in range(heads):
        q = q_ref[:, head(h)]
        both = jnp.concatenate([ch_ref[head(h), :], cl_ref[head(h), :]], axis=0)
        mix_ref[:, head(h)] = within_ref[:, head(h)] + dot(beside(q, q), both, 1, 0)
    for load in loads:
        load.wait()
    length, width = held[0].shape[1:]
    chip, core = place_ref[0], place_ref[1]
    chips = w_ref.shape[1] // (2 * width)
    grad_normed = jnp.zeros((length, width), f32)
    for ref, part in zip(held, parts):
        for b, (steps, swapped, which) in enumerate(part):
            side = 1 - core if swapped else core
            source = lax.rem(chip + chips + (2 * side - 1) * steps, chips)
            at = 2 * source + (side if which is None else which)
            columns = pl.ds(pl.multiple_of(at * width, width), width)
            grad_normed = grad_normed + dot(ref[b], w_ref[:, columns], 1, 1)
    per = DH // rows
    gains = []
    for h in range(heads):
        mixture = mix_ref[:, head(h)]
        inverse = lax.rsqrt(jnp.mean(mixture * mixture, axis=-1, keepdims=True) + 1e-06)
        part = grad_normed[:, head(h)]
        gains.append(jnp.sum(part * (mixture * inverse), axis=0, keepdims=True))
        gained = part * gain_ref[h : h + 1, :]
        inner = jnp.mean(gained * mixture, axis=-1, keepdims=True)
        grad_mixture = inverse * gained - mixture * (inverse * inverse * inverse * inner)
        high, low = halves(grad_mixture)
        high_ref[:, head(h)] = high
        low_ref[:, head(h)] = low
        q = q_ref[:, head(h)]
        outer = dot(q, beside(high, low), 0, 0)
        outer = outer[:, :DH] + outer[:, DH:]
        for at in range(0, DH, heads):
            out_ref[h * per + at // rows, at % rows // heads] = outer[at : at + heads, :]
    gain = jnp.concatenate(gains, axis=0)
    out_ref[:, rows // heads] = jnp.broadcast_to(gain[None], (heads * per, heads, DH))


def local_kernel(
    q_ref, k_ref, v_ref, ch_ref, cl_ref, mix_ref, gain_ref, gh_ref, gl_ref, att_ref, gq_ref, gk_ref, gv_ref, *, heads, self_scale
):
    for h in range(heads):
        mixture = mix_ref[:, head(h)]
        inverse = lax.rsqrt(jnp.mean(mixture * mixture, axis=-1, keepdims=True) + 1e-06)
        att_ref[:, head(h)] = (mixture * inverse * gain_ref[h : h + 1, :]).astype(bf16)
        q, k, v = q_ref[:, head(h)], k_ref[:, head(h)], v_ref[:, head(h)]
        high, low = gh_ref[:, head(h)], gl_ref[:, head(h)]
        causal, (m_high, m_low) = masked_scores(q, k, self_scale)
        scores = jnp.where(causal, dot(high, v, 1, 1) + dot(low, v, 1, 1), 0.0) * self_scale
        s_high, s_low = halves(scores)
        c_high, c_low = ch_ref[head(h), :], cl_ref[head(h), :]
        grad_query = dot(s_high, k, 1, 0) + dot(s_low, k, 1, 0)
        grad_query = grad_query + dot(high, c_high, 1, 1) + dot(high, c_low, 1, 1) + dot(low, c_high, 1, 1)
        gq_ref[:, head(h)] = grad_query.astype(bf16)
        gk_ref[:, head(h)] = dot(s_high, q, 0, 0) + dot(s_low, q, 0, 0)
        gv_ref[:, head(h)] = dot(m_high, high, 0, 0) + dot(m_high, low, 0, 0) + dot(m_low, high, 0, 0)


def suffix_kernel(in_ref, out_ref, gain_ref, *, count, rows, heads, self_scale, cross_scale):
    tiles = rows // heads
    gain = in_ref[0, tiles]
    for j in range(1, count):
        gain = gain + in_ref[j, tiles]
    gain_ref[...] = gain
    for tile in range(tiles):
        at = tile * heads
        state = jnp.zeros((heads, DH), f32)
        for j in range(count):
            out_ref[j, at : at + heads, :] = state * self_scale
            state = state + in_ref[j, tile]
        total = state * cross_scale
        for j in range(count):
            out_ref[j, rows + at : rows + at + heads, :] = total


def final_kernel(
    k_ref, v_ref, sk_ref, sv_ref, s_ref, gk_ref, gv_ref, k_hbm, v_hbm, sk_hbm, sv_hbm, out_k, out_v, out_sk, out_sv, sems, *, heads, rows
):
    per = DH // rows
    pairs = ((out_k, k_hbm), (out_v, v_hbm), (out_sk, sk_hbm), (out_sv, sv_hbm))
    stores = [pltpu.make_async_copy(a, b, sems.at[i]) for i, (a, b) in enumerate(pairs)]
    both = []
    for h in range(heads):
        later = s_ref[h * per : (h + 1) * per, :rows, :].reshape(DH, DH)
        total = s_ref[h * per : (h + 1) * per, rows:, :].reshape(DH, DH)
        both.append((head(h), *halves(later), *halves(total)))
    for at, l_high, l_low, _, _ in both:
        v = v_ref[:, at]
        out_k[:, at] = (gk_ref[:, at] + dot(beside(v, v), beside(l_high, l_low), 1, 1)).astype(bf16)
    stores[0].start()
    for at, l_high, l_low, _, _ in both:
        k = k_ref[:, at]
        out_v[:, at] = (gv_ref[:, at] + dot(beside(k, k), jnp.concatenate([l_high, l_low], axis=0), 1, 0)).astype(bf16)
    stores[1].start()
    for at, _, _, t_high, t_low in both:
        sv = sv_ref[:, at]
        out_sk[:, at] = (dot(beside(sv, sv), beside(t_high, t_low), 1, 1)).astype(bf16)
    stores[2].start()
    for at, _, _, t_high, t_low in both:
        sk = sk_ref[:, at]
        out_sv[:, at] = (dot(beside(sk, sk), jnp.concatenate([t_high, t_low], axis=0), 1, 0)).astype(bf16)
    stores[3].start()
    for store in stores:
        store.wait()


WHOLE = pl.BlockSpec(memory_space=pltpu.VMEM)
SCALAR = pl.BlockSpec(memory_space=pltpu.SMEM)
ANY = pl.BlockSpec(memory_space=pl.ANY)
HBM = pl.BlockSpec(memory_space=pltpu.HBM)


MICROSECONDS = {"states": 40, "pack": 40, "within": 40, "narrow": 40, "cotangent": 3, "local": 3}


def call(kernel, outs, name, ins=None, scratch=(), aliases=None, out_specs=None, **static):
    shapes = [jax.ShapeDtypeStruct(shape, dtype) for shape, dtype in outs]

    def run(*operands):
        return pl.pallas_call(
            functools.partial(kernel, **static),
            out_shape=shapes,
            in_specs=ins or [WHOLE] * len(operands),
            out_specs=out_specs or [WHOLE] * len(shapes),
            scratch_shapes=scratch,
            input_output_aliases=aliases or {},
            compiler_params=pltpu.CompilerParams(vmem_limit_bytes=12 * MIB),
            name=name,
            cost_estimate=pl.CostEstimate(flops=int(MICROSECONDS.get(name, 0.5) * 1e9), transcendentals=0, bytes_accessed=int(MICROSECONDS.get(name, 0.5) * 3.69e6)),
        )(*operands)

    return run


def pack(parts, after):
    shape = (sum(part.shape[0] for part in parts), *parts[0].shape[1:])
    return call(
        pack_kernel,
        [(shape, parts[0].dtype)],
        "pack",
        ins=[ANY] * (len(parts) + 1),
        scratch=[pltpu.SemaphoreType.DMA((len(parts),))],
    )(*parts, after)[0]


def gate(x, *after):
    outs = [(x.shape, x.dtype)]
    return call(gate_kernel, outs, "gate", ins=[ANY] * (1 + len(after)), aliases={0: 0}, out_specs=[ANY])(x, *after)[0]


def on_device(queries, keys, values, src_keys, src_values, norm_gain, out_weight, grad_out):
    length, width = queries.shape
    src_length = src_keys.shape[0]
    heads = width // DH
    count = lax.axis_size("seq")
    groups = lax.axis_size("heads")
    rows = width // count
    self_scale = 1.0 / math.sqrt(DH * length * count)
    cross_scale = 1.0 / math.sqrt(DH * src_length * count)
    gain = norm_gain.reshape(heads, DH)
    backwards = [list(range(count - 1, -1, -1))]

    chips = groups // 2
    chip = lax.axis_index("heads") // 2
    core = lax.axis_index("heads") % 2
    place = jnp.stack([chip, core]).astype(jnp.int32)

    def along(d):
        return [(2 * y + c, 2 * ((y + (d if c == 0 else -d)) % chips) + c) for y in range(chips) for c in range(2)]

    across = lax.ppermute(grad_out[None], "heads", along(4))
    (own,) = call(
        states_kernel,
        [((count, 2 * rows, DH), f32)],
        "states",
        ins=[HBM] * 4,
        scratch=[pltpu.VMEM(x.shape, x.dtype) for x in (keys, values, src_keys, src_values)] + [pltpu.SemaphoreType.DMA((4,))],
        heads=heads,
        rows=rows,
    )(*(pltpu.with_memory_space_constraint(x, pltpu.HBM) for x in (keys, values, src_keys, src_values)))
    held = pack([grad_out[None], across], grad_out)
    second, above, below = (lax.ppermute(held, "heads", along(d)) for d in (2, 1, -1))
    own = lax.all_to_all(own, "seq", 0, 0)
    (before,) = call(
        prefix_kernel, [((count, rows, DH), f32)], "prefix", count=count, rows=rows, self_scale=self_scale, cross_scale=cross_scale
    )(own)
    (within,) = call(
        within_kernel, [((length, width), f32)], "within", ins=[WHOLE] * 3 + [ANY], heads=heads, self_scale=self_scale
    )(queries, keys, values, before)
    second, above, below = (gate(x, within) for x in (second, above, below))
    whole = jnp.concatenate([held, second, above, below], axis=0)
    other = lax.ppermute(whole, "heads", [(i, i ^ 1) for i in range(groups)])
    before = lax.all_to_all(before, "seq", 0, 0).reshape(width, DH)
    narrow = call(narrow_kernel, [((width, DH), bf16)] * 2, "narrow")(before)
    blocks = [whole, other]
    parts = [[(d, swapped, None) for d in steps] for swapped in (False, True) for steps in ((0, 4, 2, 6, 1, 5, 7, 3),)]
    outer, g_high, g_low, mixture = call(
        cotangent_kernel,
        [((count, rows // heads + 1, heads, DH), f32), ((length, width), bf16), ((length, width), bf16), ((length, width), f32)],
        "cotangent",
        ins=[SCALAR] + [WHOLE] * len(blocks) + [HBM, HBM] + [WHOLE] * 4,
        scratch=[pltpu.VMEM(x.shape, x.dtype) for x in (out_weight, gain)] + [pltpu.SemaphoreType.DMA((9,))],
        heads=heads,
        rows=rows,
        parts=parts,
    )(place, *blocks, *(pltpu.with_memory_space_constraint(x, pltpu.HBM) for x in (out_weight, gain)), queries, within, *narrow)
    outer = lax.all_to_all(outer, "seq", 0, 0, axis_index_groups=backwards)
    attended, grad_query, grad_key, grad_value = call(
        local_kernel,
        [((length, width), bf16), ((length, width), bf16), ((length, width), f32), ((length, width), f32)],
        "local",
        heads=heads,
        self_scale=self_scale,
    )(queries, keys, values, *narrow, mixture, gain, g_high, g_low)
    later, grad_gain = call(
        suffix_kernel,
        [((count, 2 * rows, DH), f32), ((heads, DH), f32)],
        "suffix",
        count=count,
        rows=rows,
        heads=heads,
        self_scale=self_scale,
        cross_scale=cross_scale,
    )(outer)
    later = lax.all_to_all(later, "seq", 0, 0, axis_index_groups=backwards)
    shapes = [((length, width), bf16)] * 2 + [((src_length, width), bf16)] * 2
    grad_key, grad_value, grad_src_key, grad_src_value = call(
        final_kernel,
        shapes,
        "final",
        out_specs=[HBM] * 4,
        scratch=[pltpu.VMEM(*shape) for shape in shapes] + [pltpu.SemaphoreType.DMA((4,))],
        heads=heads,
        rows=rows,
    )(keys, values, src_keys, src_values, later, grad_key, grad_value)
    return attended, grad_query, grad_key, grad_value, grad_src_key, grad_src_value, grad_gain.reshape(width)


def solution(mesh):
    block = P("seq", "heads")
    return jax.shard_map(
        on_device,
        mesh=mesh,
        in_specs=(block, block, block, block, block, P("heads"), P("heads", None), block),
        out_specs=(block, block, block, block, block, block, P("heads")),
        check_vma=False,
    )
```
